128 devices in a mesh: dp: 16 (over z_hi, x, core), tp: 8 (over y, z_lo).
Axes of the slice: x: 4, y: 4, z: 4 (z_hi: 2, z_lo: 2; z = z_hi * 2 + z_lo), core: 2. Of those that a mesh axis runs over, the one named last changes fastest.
Arguments:
- hidden: bfloat16 [16384, 8192], P('dp', 'tp'), may hold values from -6 to 6
- norm_gain: float32 [8192], replicated, may hold values from 0.1 to 1.9
- lengths: int32 [32], P('dp'), may hold values from 1 to 512, 12288 in all
- query_weight: bfloat16 [8192, 8192], P('dp', 'tp'), may hold values from -0.0625 to 0.0625
- keyval_weight: bfloat16 [8192, 8, 2, 128], P('dp', 'tp'), may hold values from -0.0625 to 0.0625
Outputs:
- attended: bfloat16 [16384, 8192], P('dp', 'tp')
The draws below stay inside these ranges and needn't reach their ends.
Inputs may be any that keep to these rules, and one draw needn't show every extreme that they name: `lengths`: each rollout has 1 to 512 live tokens, they sum to 12288, and some rollout has exactly 512.
All inputs are finite; a program needn't handle non-finite values. No bound on the sum of `lengths` on one device may be relied on, other than what follows from the above.
Results may differ from the reference program's by a relative error of at most 0.0085.
Values may be sent and summed in bfloat16 or wider, within the bound.
No kernel may reach another device: no remote copies, remote signals or barrier semaphores. Data moves between devices by JAX's collectives and lax.ppermute only.
A program may use at most 128 MiB of HBM per device.

```python
import math
import jax
import jax.numpy as jnp
import numpy as np
from jax import lax

D = 8192
H = 64
KVH = 8
HD = 128
LEN = 512
SEQS = 32
TOKENS = 16384


def level_of(rng, extent, shards, smallest, largest):
    gain, own = 1.0, jax.random.fold_in(rng, 6)
    for axis_at, shards_of in shards:
        heights = jnp.exp(jax.random.uniform(jax.random.fold_in(own, axis_at), (shards_of,), jnp.float32, smallest / len(shards), largest / len(shards)))
        gain = gain * jnp.repeat(heights, extent[axis_at] // shards_of).reshape([-1 if axis == axis_at else 1 for axis in range(len(extent))])
    return gain


def length_profile(count, total, most, lean):
    portions = [(1 << 20) // math.isqrt(rank ** lean) + 1 for rank in range(2, count + 1)]
    spare, given = total - most - (count - 1), [1] * (count - 1)
    while spare > 0:
        free = [i for i in range(count - 1) if given[i] < most]
        whole, budget = sum([portions[i] for i in free]), spare
        for i in free:
            more = min(most - given[i], max(1, budget * portions[i] // whole), spare)
            given[i] = given[i] + more
            spare = spare - more
    return np.array([most] + given)


def uneven_parts(rng, amount, total, reach, slope):
    if amount == 2:
        one = jax.random.randint(rng, (), max(1, total - reach), min(reach, total - 1) + 1)
        return jnp.stack([one, total - one])
    tallies = jnp.asarray(length_profile(amount, total, reach, slope), jnp.int32)
    twos = (amount - 1) // 2
    source_of, receiver = tallies[1:1 + 2 * twos:2], tallies[2:2 + 2 * twos:2]
    slack = jnp.minimum(source_of - 1, reach - receiver)
    passed = jax.random.randint(jax.random.fold_in(rng, 1), (twos,), 0, 1 << 20) % (slack + 1)
    tallies = tallies.at[1:1 + 2 * twos:2].set(source_of - passed).at[2:2 + 2 * twos:2].set(receiver + passed)
    return tallies[jax.random.permutation(jax.random.fold_in(rng, 2), amount)]


def bell_draw(rng, shape, scale, reach, cuts=(), kind=jnp.bfloat16):
    factor_of = level_of(rng, shape, cuts, -0.22, 0.18) if cuts else 1.0
    drawn = jax.random.normal(rng, shape, jnp.float32) * scale * factor_of
    return jnp.minimum(jnp.maximum(drawn, -reach), reach).astype(kind)


def setup_inputs(seed: int = 0) -> dict:
    key_list = jax.random.split(jax.random.key(seed), 6)
    return {
        "hidden": bell_draw(key_list[0], (TOKENS, D), 1.0, 6.0, ((0, 16), (1, 8))),
        "norm_gain": jnp.clip(1.0 + 0.18 * jax.random.normal(key_list[1], (D,), jnp.float32), 0.1, 1.9),
        "lengths": uneven_parts(key_list[2], SEQS, SEQS * (3 * LEN // 4), LEN, 2).astype(jnp.int32),
        "query_weight": bell_draw(key_list[3], (D, H * HD), D ** -0.5, 0.0625, ((0, 16), (1, 8))),
        "keyval_weight": bell_draw(key_list[4], (D, KVH, 2, HD), D ** -0.5, 0.0625, ((0, 16), (1, 8))),
    }


def attend_one(query, keyval, length):
    keys = keyval[:, :, 0].astype(jnp.float32)
    values = keyval[:, :, 1].astype(jnp.float32)
    span = query.shape[0]
    scale = query.shape[-1] ** (-0.5)
    scores = jnp.einsum('qkgd,jkd->kgqj', query.astype(jnp.float32), keys) * scale
    rowpos = lax.broadcasted_iota(jnp.int32, (span, span), 0)
    colpos = lax.broadcasted_iota(jnp.int32, (span, span), 1)
    allowed = (colpos <= rowpos) & (colpos < length)
    scores = jnp.where(allowed, scores, -jnp.inf)
    peak = lax.optimization_barrier(jnp.max(scores, axis=-1, keepdims=True))
    expo = jnp.exp(scores - peak)
    probs = (expo / lax.optimization_barrier(jnp.sum(expo, axis=-1, keepdims=True))).astype(jnp.bfloat16)
    mixed = jnp.einsum('kgqj,jkd->qkgd', probs.astype(jnp.float32), values)
    return mixed.astype(jnp.bfloat16)

def reference(hidden, norm_gain, lengths, query_weight, keyval_weight):
    widened = hidden.astype(jnp.float32)
    meansq = lax.optimization_barrier(jnp.mean(widened * widened, axis=-1, keepdims=True))
    normed = (widened * lax.rsqrt(meansq + 1e-05) * norm_gain).astype(jnp.bfloat16)
    query = jnp.dot(normed, query_weight, preferred_element_type=jnp.float32).astype(jnp.bfloat16)
    keyval = jnp.dot(normed, keyval_weight.reshape(D, -1), preferred_element_type=jnp.float32).astype(jnp.bfloat16)
    seq_count = lengths.shape[0]
    query = query.reshape(seq_count, LEN, KVH, H // KVH, HD)
    keyval = keyval.reshape(seq_count, LEN, KVH, 2, HD)
    mixed = lax.map(lambda item: attend_one(item[0], item[1], item[2]), (query, keyval, lengths))
    return mixed.reshape(seq_count * LEN, H * HD)
```

```python
import jax
import jax.numpy as jnp
from jax import lax
from jax.experimental import pallas as pl
from jax.experimental.pallas import tpu as pltpu
from jax.sharding import Mesh, PartitionSpec as P

LOG2E = 1.4426950408889634
HEAD = 128
GROUPS = 8
EPS = 1e-05


def ring(a, axis):
    perm = []
    for c in range(2):
        for i in range(4):
            j = (i + 1) % 4 if c == 0 else (i - 1) % 4
            if axis == "y":
                perm.append((c * 4 + i, c * 4 + j))
            else:
                perm.append((i * 2 + c, j * 2 + c))
    return lax.ppermute(a, ("c", "y") if axis == "y" else ("x", "c"), perm)


def swap(a, axis):
    return lax.ppermute(a, axis, [(0, 1), (1, 0)])


def circle(a, axis):
    got = [a]
    for _ in range(3):
        got.append(ring(got[-1], axis))
    return got


def gate(a, *after):
    return lax.optimization_barrier((a, *after))[0]


def empty(shape, dtype):
    return pl.pallas_call(
        lambda out: None,
        out_shape=jax.ShapeDtypeStruct(shape, dtype),
        out_specs=pl.BlockSpec(memory_space=pl.ANY),
    )()


def attend_kernel(length_ref, inv_ref, q_ref, k_ref, v_ref, out_ref):
    length = length_ref[0]
    span = q_ref.shape[0]
    half = span // 2
    inv = inv_ref[...]
    q = (q_ref[...] * inv).astype(jnp.bfloat16)
    k = (k_ref[...] * inv).astype(jnp.bfloat16)
    v = (v_ref[...] * inv).astype(jnp.bfloat16)
    factor = LOG2E * HEAD**-0.5
    for part in range(2):
        lo, hi = part * half, (part + 1) * half
        s = lax.dot_general(
            q[lo:hi], k[:hi], (((1,), (1,)), ((), ())), preferred_element_type=jnp.float32
        )
        row = lax.broadcasted_iota(jnp.int32, s.shape, 0) + lo
        col = lax.broadcasted_iota(jnp.int32, s.shape, 1)
        s = jnp.where((col <= row) & (col < length), s, -jnp.inf)
        peak = jnp.max(s, axis=-1, keepdims=True)
        e = jnp.exp2((s - peak) * factor)
        total = jnp.sum(e, axis=-1, keepdims=True)
        mixed = jnp.dot(e.astype(jnp.bfloat16), v[:hi], preferred_element_type=jnp.float32)
        out_ref[lo:hi, :] = (mixed / total).astype(jnp.bfloat16)


def attend(acc, inv, length):
    span = acc.shape[0]
    return pl.pallas_call(
        attend_kernel,
        grid=(GROUPS,),
        in_specs=[
            pl.BlockSpec(memory_space=pltpu.SMEM),
            pl.BlockSpec((span, 1), lambda g: (0, 0)),
            pl.BlockSpec((span, HEAD), lambda g: (0, g)),
            pl.BlockSpec((span, HEAD), lambda g: (0, GROUPS)),
            pl.BlockSpec((span, HEAD), lambda g: (0, GROUPS + 1)),
        ],
        out_specs=pl.BlockSpec((span, HEAD), lambda g: (0, g)),
        out_shape=jax.ShapeDtypeStruct((span, GROUPS * HEAD), jnp.bfloat16),
        cost_estimate=pl.CostEstimate(flops=10**9, bytes_accessed=4 * 10**6, transcendentals=2 * 10**6),
    )(length, inv, acc, acc, acc)


def local(hidden, norm_gain, lengths, query_weight, keyval_weight):
    zh, x, c = lax.axis_index("zh"), lax.axis_index("x"), lax.axis_index("c")
    y, zl = lax.axis_index("y"), lax.axis_index("zl")
    rows, feats = query_weight.shape[0], hidden.shape[1]

    gain = lax.dynamic_slice(norm_gain, ((zh * 8 + x * 2 + c) * rows,), (rows,))
    own = jnp.concatenate([query_weight, keyval_weight.reshape(rows, -1)], axis=1)
    own = (own.astype(jnp.float32) * gain[:, None]).astype(jnp.bfloat16)
    width = own.shape[1]

    wide = hidden.astype(jnp.float32)
    square = lax.psum(jnp.sum(wide * wide, axis=-1, keepdims=True), ("y", "zl"))
    inv = lax.rsqrt(square / (feats * 8) + EPS)

    span = hidden.shape[0] // 2
    half = span // 2
    h0, h1, h2 = hidden[:span], hidden[span : span + half], hidden[span + half :]

    own0, own2 = circle(h0, "y"), circle(h2, "y")
    far = swap(own, "zh")
    h0_far = swap(gate(h0, far), "zl")
    h2_far = [swap(gate(h2, h0_far), "zl")]
    h1_far = swap(gate(h1, h2_far[0]), "zl")
    last = h1_far
    for a in own2[1:]:
        last = swap(gate(a, last), "zl")
        h2_far.append(last)
    far0 = circle(gate(h0_far, own0[3]), "y")
    own1 = [h1, ring(gate(h1, own2[3]), "y")]
    own1.append(ring(gate(own1[1], far0[2]), "y"))
    far1 = [h1_far, ring(gate(h1_far, far0[3]), "y")]
    own1.append(ring(own1[2], "y"))
    far1.append(ring(far1[1], "y"))
    far1.append(ring(far1[2], "y"))

    near_w = circle(own, "x")
    far_w = circle(gate(far, near_w[3]), "x")
    whole = empty((16 * rows, width), jnp.bfloat16)
    for got, z_of in ((near_w, zh), (far_w, 1 - zh)):
        for k, a in enumerate(got):
            up, down = (x - k) & 3, (x + k) & 3
            here, there = jnp.where(c == 0, up, down), jnp.where(c == 0, down, up)
            at = ((z_of * 8 + here * 2 + c) * rows, 0)
            whole = lax.dynamic_update_slice(whole, a, at)
            at = ((z_of * 8 + there * 2 + 1 - c) * rows, 0)
            whole = lax.dynamic_update_slice(whole, swap(a, "c"), at)

    def project(parts):
        acc = None
        for got, z_of in parts:
            for k, a in enumerate(got):
                at = (jnp.where(c == 0, y - k, y + k) & 3) * 2 + z_of
                w = lax.dynamic_slice(whole, (at * feats, 0), (feats, width))
                add = jnp.dot(a, w, preferred_element_type=jnp.float32)
                acc = add if acc is None else acc + add
        return acc

    out0 = attend(project(((own0, zl), (far0, 1 - zl))), inv[:span], lengths[:1])
    acc2 = project(((own2, zl), (h2_far, 1 - zl)))
    acc1 = project(((own1, zl), (far1, 1 - zl)))
    acc = jnp.concatenate([acc1, acc2], axis=0)
    out1 = attend(acc, inv[span:], lengths[1:])
    return jnp.concatenate([out0, out1], axis=0)


def solution(mesh):
    fine = Mesh(mesh.devices.reshape(2, 4, 2, 4, 2), ("zh", "x", "c", "y", "zl"))
    dp, tp = ("zh", "x", "c"), ("y", "zl")
    in_specs = (P(dp, tp), P(), P(dp), P(dp, tp), P(dp, tp, None, None))
    return jax.shard_map(local, mesh=fine, in_specs=in_specs, out_specs=P(dp, tp), check_vma=False)
```

```python
import jax
import jax.numpy as jnp
from jax import lax
from jax.experimental import pallas as pl
from jax.experimental.pallas import tpu as pltpu
from jax.sharding import Mesh, PartitionSpec as P

LOG2E = 1.4426950408889634
HEAD = 128
GROUPS = 8
EPS = 1e-05


def ring(a, axis, sign=1):
    perm = []
    for c in range(2):
        for i in range(4):
            j = (i + sign) % 4 if c == 0 else (i - sign) % 4
            if axis == "y":
                perm.append((c * 4 + i, c * 4 + j))
            else:
                perm.append((i * 2 + c, j * 2 + c))
    return lax.ppermute(a, ("c", "y") if axis == "y" else ("x", "c"), perm)


def swap(a, axis):
    return lax.ppermute(a, axis, [(0, 1), (1, 0)])


def flip(a, axis, bit):
    size = 4 if axis == "y" else 2
    return lax.ppermute(a, axis, [(i, i ^ bit) for i in range(size)])


def together(*arrays):
    return lax.optimization_barrier(arrays)


def attend_block(acc, inv, length, out_ref):
    span = acc.shape[0]
    half = span // 2
    factor = LOG2E * HEAD**-0.5
    at_k, at_v = GROUPS * HEAD, (GROUPS + 1) * HEAD
    k = (acc[:, at_k : at_k + HEAD] * inv).astype(jnp.bfloat16)
    v = (acc[:, at_v : at_v + HEAD] * inv).astype(jnp.bfloat16)
    v = jnp.concatenate([v, jnp.ones_like(v)], axis=1)
    for part in range(2):
        lo, hi = part * half, (part + 1) * half
        row = lax.broadcasted_iota(jnp.int32, (half, hi), 0) + lo
        col = lax.broadcasted_iota(jnp.int32, (half, hi), 1)
        bias = jnp.where((col <= row) & (col < length), 0.0, -jnp.inf)
        for g in range(GROUPS):
            at = slice(g * HEAD, (g + 1) * HEAD)
            q = (acc[lo:hi, at] * inv[lo:hi]).astype(jnp.bfloat16)
            s = lax.dot_general(
                q, k[:hi], (((1,), (1,)), ((), ())), preferred_element_type=jnp.float32
            )
            s = s + bias
            peak = jnp.max(s, axis=-1, keepdims=True)
            e = jnp.exp2((s - peak) * factor).astype(jnp.bfloat16)
            mixed = jnp.dot(e, v[:hi], preferred_element_type=jnp.float32)
            out_ref[lo:hi, at] = (mixed[:, :HEAD] / mixed[:, HEAD:]).astype(jnp.bfloat16)


def stage(parts, sel, weights, acc_in=None, final=None):
    flat, where = [], []
    for part in parts:
        spots = []
        for array, row, count in part:
            known = [i for i, have in enumerate(flat) if have is array]
            if not known:
                flat.append(array)
            spots.append((known[0] if known else len(flat) - 1, row, count))
        where.append(spots)
    n = len(parts)
    rows = sum(count for _, _, count in where[0])
    feats = flat[0].shape[1]
    deep, width = weights[0].shape
    extra = [] if acc_in is None else [acc_in]
    if final is not None:
        inv, length, out_row, out_old = final
        extra += [inv, length] + ([] if out_old is None else [out_old])

    def body(sel_ref, *refs):
        refs = list(refs)
        pieces = [refs.pop(0) for _ in flat]
        blocks = [refs.pop(0) for _ in weights]
        acc_ref = None if acc_in is None else refs.pop(0)
        if final is not None:
            inv_ref, length_ref = refs.pop(0), refs.pop(0)
            if out_old is not None:
                refs.pop(0)
        out_ref = refs.pop(0)
        a_buf, w_buf, acc, sem_a, sem_w, sem_c = refs[:6]

        def fetch(k, slot):
            for j, spots in enumerate(where):
                @pl.when(k == j)
                def _(spots=spots):
                    to = 0
                    for i, row, count in spots:
                        pltpu.make_async_copy(
                            pieces[i].at[pl.ds(row, count)], a_buf.at[slot, pl.ds(to, count)], sem_a.at[slot]
                        ).start()
                        to += count
            for side in range(2):
                for j, block in enumerate(blocks):
                    @pl.when(sel_ref[2 * k + side] == j)
                    def _(block=block, side=side):
                        pltpu.make_async_copy(
                            block, w_buf.at[slot, pl.ds(side * deep, deep)], sem_w.at[slot]
                        ).start()

        fetch(0, 0)
        if acc_ref is not None:
            load = pltpu.make_async_copy(acc_ref, acc, sem_c)
            load.start()
            load.wait()
        else:
            acc[...] = jnp.zeros_like(acc)

        def step(k, carry):
            slot = lax.rem(k, 2)

            @pl.when(k + 1 < n)
            def _():
                fetch(k + 1, 1 - slot)

            pltpu.make_async_copy(a_buf.at[slot], a_buf.at[slot], sem_a.at[slot]).wait()
            pltpu.make_async_copy(w_buf.at[slot], w_buf.at[slot], sem_w.at[slot]).wait()
            for tile in range(0, width, 256):
                at = slice(tile, tile + 256)
                acc[:, at] += jnp.dot(a_buf[slot], w_buf[slot, :, at], preferred_element_type=jnp.float32)
            return carry

        lax.fori_loop(0, n, step, 0)
        if final is None:
            save = pltpu.make_async_copy(acc, out_ref, sem_c)
        else:
            done = refs[6]
            attend_block(acc, inv_ref[...], length_ref[0], done)
            save = pltpu.make_async_copy(done, out_ref.at[pl.ds(out_row, rows)], sem_c)
        save.start()
        save.wait()

    anywhere = pl.BlockSpec(memory_space=pl.ANY)
    smem = pl.BlockSpec(memory_space=pltpu.SMEM)
    specs = [smem] + [anywhere] * (len(flat) + len(weights) + (acc_in is not None))
    scratch = [
        pltpu.VMEM((2, rows, feats), jnp.bfloat16),
        pltpu.VMEM((2, 2 * deep, width), jnp.bfloat16),
        pltpu.VMEM((rows, width), jnp.float32),
        pltpu.SemaphoreType.DMA((2,)),
        pltpu.SemaphoreType.DMA((2,)),
        pltpu.SemaphoreType.DMA,
    ]
    aliases = {}
    flops = 2 * n * rows * feats * width
    if final is None:
        out = jax.ShapeDtypeStruct((rows, width), jnp.float32)
    else:
        specs += [pl.BlockSpec(memory_space=pltpu.VMEM), smem]
        out = jax.ShapeDtypeStruct((2 * rows, GROUPS * HEAD), jnp.bfloat16)
        scratch.append(pltpu.VMEM((rows, GROUPS * HEAD), jnp.bfloat16))
        flops += 6 * 10**9
        if out_old is not None:
            aliases[len(specs)] = 0
            specs.append(anywhere)
    return pl.pallas_call(
        body,
        in_specs=specs,
        out_specs=anywhere,
        out_shape=out,
        scratch_shapes=scratch,
        input_output_aliases=aliases,
        compiler_params=pltpu.CompilerParams(vmem_limit_bytes=30 << 20),
        cost_estimate=pl.CostEstimate(flops=flops, bytes_accessed=n * 4 * 10**6, transcendentals=0),
    )(sel, *flat, *weights, *extra)


def local(hidden, norm_gain, lengths, query_weight, keyval_weight):
    zh, x, c = lax.axis_index("zh"), lax.axis_index("x"), lax.axis_index("c")
    y, zl = lax.axis_index("y"), lax.axis_index("zl")
    rows, feats = query_weight.shape[0], hidden.shape[1]
    span = hidden.shape[0] // 2
    cut = span + span // 2

    gain = lax.dynamic_slice(norm_gain, ((zh * 8 + x * 2 + c) * rows,), (rows,))
    own = jnp.concatenate([query_weight, keyval_weight.reshape(rows, -1)], axis=1)
    own = (own.astype(jnp.float32) * gain[:, None]).astype(jnp.bfloat16)
    width = own.shape[1]

    wide = hidden.astype(jnp.float32)
    square = jnp.sum(wide * wide, axis=-1).reshape(8, -1)
    square = square + flip(square, "y", 1)

    h0 = hidden
    far = swap(own, "zh")
    h1 = ring(h0, "y")
    w1, w3 = ring(own, "x"), ring(own, "x", -1)
    v0 = swap(own, "c")
    h0, w0, h1, w1, w3, f0, square = together(h0, own, h1, w1, w3, far, square)
    square = square + flip(square, "y", 2)
    h3 = ring(h0, "y", -1)
    lo0 = swap(h0[:span], "zl")
    w2, f1 = ring(w1, "x"), ring(f0, "x")
    v1, v3 = swap(w1, "c"), swap(w3, "c")
    h0, h1, h3, lo0, w2, f0, f1, square = together(h0, h1, h3, lo0, w2, f0, f1, square)
    square = square + flip(square, "zl", 1)
    h2a = ring(h1[:cut], "y")
    lo1 = ring(lo0, "y")
    hi0 = swap(h0[span:], "zl")
    f3, f2 = ring(f0, "x", -1), ring(f1, "x")
    v2, g0, g1 = swap(w2, "c"), swap(f0, "c"), swap(f1, "c")
    h1, h3, h2a, lo0, lo1, hi0, f3, f2 = together(h1, h3, h2a, lo0, lo1, hi0, f3, f2)
    g3, g2 = swap(f3, "c"), swap(f2, "c")
    lo2, lo3 = ring(lo1, "y"), ring(lo0, "y", -1)
    tails = swap(jnp.concatenate([h1[span:cut], h3[span:cut]], axis=0), "zl")
    weights = [w0, w1, w2, w3, v0, v1, v2, v3, f0, f1, f2, f3, g0, g1, g2, g3]
    half = span // 2

    def choose(*ones):
        step = jnp.array([k for k, _ in ones], jnp.int32)
        other = jnp.array([z for _, z in ones], jnp.int32)
        b = 2 * (jnp.where(c == 0, y - step, y + step) & 3) + (zl ^ other)
        z_at, x_at = b >> 2, b & 3
        core = jnp.array([0, 1], jnp.int32)[None, :]
        k = jnp.where(core == 0, x - x_at[:, None], x_at[:, None] - x) & 3
        return (((z_at ^ zh)[:, None]) * 8 + (core ^ c) * 4 + k).reshape(-1)

    first = [(h0, 0, span)], [(h1, 0, span)], [(h2a, 0, span)], [(h3, 0, span)], [(lo0, 0, span)], [(lo1, 0, span)]
    acc0 = stage(first, choose((0, 0), (1, 0), (2, 0), (3, 0), (0, 1), (1, 1)), weights)
    lo2, lo3, tails, h1, h2a, hi0, acc0 = together(lo2, lo3, tails, h1, h2a, hi0, acc0)
    h2b = ring(h1[cut:], "y")
    mid0 = hi0[half:]
    mid1, mid3 = ring(mid0, "y"), ring(mid0, "y", -1)
    tail2 = swap(h2a[span:], "zl")
    inv = lax.rsqrt(square.reshape(-1, 1) / (feats * 8) + EPS)
    out = stage(
        ([(lo2, 0, span)], [(lo3, 0, span)]), choose((2, 1), (3, 1)), weights, acc0, (inv[:span], lengths[:1], 0, None)
    )
    parts = [(h0, span, span)], [(h1, span, span)], [(h3, span, span)], [(hi0, 0, span)]
    acc1 = stage(parts, choose((0, 0), (1, 0), (3, 0), (0, 1)), weights)
    h2b, mid1, mid3, tail2, acc1, out = together(h2b, mid1, mid3, tail2, acc1, out)
    mid2 = ring(mid1, "y")
    parts = [(h2a, span, half), (h2b, 0, half)], [(tails, 0, half), (mid1, 0, half)], [(tails, half, half), (mid3, 0, half)]
    acc1 = stage(parts, choose((2, 0), (1, 1), (3, 1)), weights, acc1)
    parts = ([(tail2, 0, half), (mid2, 0, half)],)
    return stage(parts, choose((2, 1)), weights, acc1, (inv[span:], lengths[1:], span, out))


def solution(mesh):
    fine = Mesh(mesh.devices.reshape(2, 4, 2, 4, 2), ("zh", "x", "c", "y", "zl"))
    dp, tp = ("zh", "x", "c"), ("y", "zl")
    in_specs = (P(dp, tp), P(), P(dp), P(dp, tp), P(dp, tp, None, None))
    return jax.shard_map(local, mesh=fine, in_specs=in_specs, out_specs=P(dp, tp), check_vma=False)
```

```python
import jax
import jax.numpy as jnp
from jax import lax
from jax.experimental import pallas as pl
from jax.experimental.pallas import tpu as pltpu
from jax.sharding import Mesh, PartitionSpec as P

LOG2E = 1.4426950408889634
HEAD = 128
GROUPS = 8
EPS = 1e-05


def ring(a, axis, sign=1):
    perm = []
    for c in range(2):
        for i in range(4):
            j = (i + sign) % 4 if c == 0 else (i - sign) % 4
            if axis == "y":
                perm.append((c * 4 + i, c * 4 + j))
            else:
                perm.append((i * 2 + c, j * 2 + c))
    return lax.ppermute(a, ("c", "y") if axis == "y" else ("x", "c"), perm)


def swap(a, axis):
    return lax.ppermute(a, axis, [(0, 1), (1, 0)])


def squares(a):
    wide = a.astype(jnp.float32)
    return jnp.sum(wide * wide, axis=-1)


def together(*arrays):
    return lax.optimization_barrier(arrays)


def attend_block(acc, inv, length, out_ref):
    span = acc.shape[0]
    half = span // 2
    factor = LOG2E * HEAD**-0.5
    at_k, at_v = GROUPS * HEAD, (GROUPS + 1) * HEAD
    k = (acc[:, at_k : at_k + HEAD] * inv).astype(jnp.bfloat16)
    v = (acc[:, at_v : at_v + HEAD] * inv).astype(jnp.bfloat16)
    v = jnp.concatenate([v, jnp.ones_like(v)], axis=1)
    for part in range(2):
        lo, hi = part * half, (part + 1) * half
        row = lax.broadcasted_iota(jnp.int32, (half, hi), 0) + lo
        col = lax.broadcasted_iota(jnp.int32, (half, hi), 1)
        bias = jnp.where((col <= row) & (col < length), 0.0, -jnp.inf)
        for g in range(GROUPS):
            at = slice(g * HEAD, (g + 1) * HEAD)
            q = (acc[lo:hi, at] * inv[lo:hi]).astype(jnp.bfloat16)
            s = lax.dot_general(
                q, k[:hi], (((1,), (1,)), ((), ())), preferred_element_type=jnp.float32
            )
            s = s + bias
            peak = jnp.max(s, axis=-1, keepdims=True)
            e = jnp.exp2((s - peak) * factor).astype(jnp.bfloat16)
            mixed = jnp.dot(e, v[:hi], preferred_element_type=jnp.float32)
            out_ref[lo:hi, at] = (mixed[:, :HEAD] / mixed[:, HEAD:]).astype(jnp.bfloat16)


def stage(parts, sel, weights, acc_in=None, final=None):
    flat, where = [], []
    for part in parts:
        spots = []
        for array, row, count in part:
            known = [i for i, have in enumerate(flat) if have is array]
            if not known:
                flat.append(array)
            spots.append((known[0] if known else len(flat) - 1, row, count))
        where.append(spots)
    n = len(parts)
    rows = sum(count for _, _, count in where[0])
    feats = flat[0].shape[1]
    deep, width = weights[0][0].shape[0], weights[0][0].shape[1]
    stores = []
    for array, _ in weights:
        if not any(have is array for have in stores):
            stores.append(array)
    spots_w = [(next(i for i, have in enumerate(stores) if have is array), row) for array, row in weights]
    extra = [] if acc_in is None else [acc_in[0]]
    if final is not None:
        inv, length, out_row, out_old = final
        extra += [inv, length] + ([] if out_old is None else [out_old])

    def body(sel_ref, *refs):
        refs = list(refs)
        pieces = [refs.pop(0) for _ in flat]
        blocks = [refs.pop(0) for _ in stores]
        acc_ref = None if acc_in is None else refs.pop(0)
        if final is not None:
            inv_ref, length_ref = refs.pop(0), refs.pop(0)
            if out_old is not None:
                refs.pop(0)
        out_ref = refs.pop(0)
        a_buf, w_buf, acc, sem_a, sem_w, sem_c = refs[:6]

        def fetch(k, slot):
            for j, spots in enumerate(where):
                @pl.when(k == j)
                def _(spots=spots):
                    to = 0
                    for i, row, count in spots:
                        pltpu.make_async_copy(
                            pieces[i].at[pl.ds(row, count)], a_buf.at[slot, pl.ds(to, count)], sem_a.at[slot]
                        ).start()
                        to += count
            for side in range(2):
                for j, (i, row) in enumerate(spots_w):
                    @pl.when(sel_ref[2 * k + side] == j)
                    def _(i=i, row=row, side=side):
                        pltpu.make_async_copy(
                            blocks[i].at[pl.ds(row, deep)], w_buf.at[slot, pl.ds(side * deep, deep)], sem_w.at[slot]
                        ).start()

        fetch(0, 0)
        if acc_ref is not None:
            load = pltpu.make_async_copy(acc_ref.at[pl.ds(acc_in[1], rows)], acc, sem_c)
            load.start()
            load.wait()
        else:
            acc[...] = jnp.zeros_like(acc)

        def step(k, carry):
            slot = lax.rem(k, 2)

            @pl.when(k + 1 < n)
            def _():
                fetch(k + 1, 1 - slot)

            pltpu.make_async_copy(a_buf.at[slot], a_buf.at[slot], sem_a.at[slot]).wait()
            pltpu.make_async_copy(w_buf.at[slot], w_buf.at[slot], sem_w.at[slot]).wait()
            for tile in range(0, width, 256):
                at = slice(tile, tile + 256)
                acc[:, at] += jnp.dot(a_buf[slot], w_buf[slot, :, at], preferred_element_type=jnp.float32)
            return carry

        lax.fori_loop(0, n, step, 0)
        if final is None:
            save = pltpu.make_async_copy(acc, out_ref, sem_c)
        else:
            done = refs[6]
            attend_block(acc, inv_ref[...], length_ref[0], done)
            save = pltpu.make_async_copy(done, out_ref.at[pl.ds(out_row, rows)], sem_c)
        save.start()
        save.wait()

    anywhere, main = pl.BlockSpec(memory_space=pl.ANY), pl.BlockSpec(memory_space=pl.ANY)
    smem = pl.BlockSpec(memory_space=pltpu.SMEM)
    specs = [smem] + [anywhere] * (len(flat) + len(stores)) + [main] * (acc_in is not None)
    scratch = [
        pltpu.VMEM((2, rows, feats), jnp.bfloat16),
        pltpu.VMEM((2, 2 * deep, width), jnp.bfloat16),
        pltpu.VMEM((rows, width), jnp.float32),
        pltpu.SemaphoreType.DMA((2,)),
        pltpu.SemaphoreType.DMA((2,)),
        pltpu.SemaphoreType.DMA,
    ]
    aliases = {}
    flops = 2 * n * rows * feats * width
    if final is None:
        out = jax.ShapeDtypeStruct((rows, width), jnp.float32)
    else:
        specs += [pl.BlockSpec(memory_space=pltpu.VMEM), smem]
        out = jax.ShapeDtypeStruct((2 * rows, GROUPS * HEAD), jnp.bfloat16)
        scratch.append(pltpu.VMEM((rows, GROUPS * HEAD), jnp.bfloat16))
        flops += 6 * 10**9
        if out_old is not None:
            aliases[len(specs)] = 0
            specs.append(main)
    return pl.pallas_call(
        body,
        in_specs=specs,
        out_specs=main,
        out_shape=out,
        scratch_shapes=scratch,
        input_output_aliases=aliases,
        compiler_params=pltpu.CompilerParams(vmem_limit_bytes=56 << 20),
        cost_estimate=pl.CostEstimate(flops=flops, bytes_accessed=n * 4 * 10**6, transcendentals=0),
    )(sel, *flat, *stores, *extra)


def local(hidden, norm_gain, lengths, query_weight, keyval_weight):
    zh, x, c = lax.axis_index("zh"), lax.axis_index("x"), lax.axis_index("c")
    y, zl = lax.axis_index("y"), lax.axis_index("zl")
    rows, feats = query_weight.shape[0], hidden.shape[1]
    span = hidden.shape[0] // 2
    cut = span + span // 2

    gain = lax.dynamic_slice(norm_gain, ((zh * 8 + x * 2 + c) * rows,), (rows,))
    own = jnp.concatenate([query_weight, keyval_weight.reshape(rows, -1)], axis=1)
    own = (own.astype(jnp.float32) * gain[:, None]).astype(jnp.bfloat16)
    width = own.shape[1]

    half = span // 2
    h0, w0 = hidden, own
    f0 = swap(w0, "zh")
    w1, w3 = ring(w0, "x"), ring(w0, "x", -1)
    h1 = ring(h0, "y")
    h_lo, h_hi = h0[:span], h0[span:]
    h3_lo = ring(h_lo, "y", -1)
    square = squares(h0)
    f0, w0, w1, w3, h0, h1, h3_lo, h_lo, h_hi, square = together(f0, w0, w1, w3, h0, h1, h3_lo, h_lo, h_hi, square)
    w2, f1 = ring(w1, "x"), ring(f0, "x")
    h3_hi = ring(h_hi, "y", -1)
    h2_lo = ring(h1[:span], "y")
    lo0 = swap(h_lo, "zl")
    others = jnp.concatenate([w0, w1, w3], axis=0)
    square += squares(h1)
    h1_hi = h1[span:]
    w2, f0, f1, h0, h1, h1_hi, h2_lo, h3_hi, lo0, h_hi, square, others = together(
        w2, f0, f1, h0, h1, h1_hi, h2_lo, h3_hi, lo0, h_hi, square, others
    )
    others = swap(others, "c")
    f3, f2 = ring(f0, "x", -1), ring(f1, "x")
    h2_hi = ring(h1_hi, "y")
    hi0 = swap(h_hi, "zl")
    lo1 = ring(lo0, "y")
    more = jnp.concatenate([w2, f0, f1], axis=0)
    square += jnp.concatenate([squares(h2_lo) + squares(h3_lo), squares(h3_hi)], axis=0)
    tail = jnp.concatenate([h1_hi[:half], h3_hi[:half]], axis=0)
    f3, f2, h2_lo, h2_hi, h3_hi, hi0, lo0, lo1, tail, square, others, more = together(
        f3, f2, h2_lo, h2_hi, h3_hi, hi0, lo0, lo1, tail, square, others, more
    )
    more = swap(more, "c")
    last = swap(jnp.concatenate([f2, f3], axis=0), "c")
    lo2, lo3 = ring(lo1, "y"), ring(lo0, "y", -1)
    mid0 = hi0[half:]
    mid1 = ring(mid0, "y")
    tails = swap(tail, "zl")
    square += jnp.concatenate([jnp.zeros_like(square[:span]), squares(h2_hi)], axis=0)
    square = square.reshape(8, -1)
    weights = [(w0, 0), (w1, 0), (w2, 0), (w3, 0), (others, 0), (others, rows), (more, 0), (others, 2 * rows)]
    weights += [(f0, 0), (f1, 0), (f2, 0), (f3, 0), (more, rows), (more, 2 * rows), (last, 0), (last, rows)]

    def choose(*ones):
        step = jnp.array([k for k, _ in ones], jnp.int32)
        other = jnp.array([z for _, z in ones], jnp.int32)
        b = 2 * (jnp.where(c == 0, y - step, y + step) & 3) + (zl ^ other)
        z_at, x_at = b >> 2, b & 3
        core = jnp.array([0, 1], jnp.int32)[None, :]
        k = jnp.where(core == 0, x - x_at[:, None], x_at[:, None] - x) & 3
        return (((z_at ^ zh)[:, None]) * 8 + (core ^ c) * 4 + k).reshape(-1)

    parts = [(h0, 0, 2 * span)], [(h1, 0, 2 * span)], [(h2_lo, 0, span), (h2_hi, 0, span)], [(h3_lo, 0, span), (h3_hi, 0, span)]
    parts += ([(lo0, 0, span), (hi0, 0, span)],)
    acc = stage(parts, choose((0, 0), (1, 0), (2, 0), (3, 0), (0, 1)), weights)
    tail = h2_hi[:half]
    lo2, lo3, mid0, mid1, tails, tail, acc, square = together(lo2, lo3, mid0, mid1, tails, tail, acc, square)
    square = square + swap(square, "zl")
    mid2, mid3 = ring(mid1, "y"), ring(mid0, "y", -1)
    tail2 = swap(tail, "zl")
    inv = lax.rsqrt(square.reshape(-1, 1) / (feats * 8) + EPS)
    parts = [(lo1, 0, span)], [(lo2, 0, span)], [(lo3, 0, span)]
    out = stage(parts, choose((1, 1), (2, 1), (3, 1)), weights, (acc, 0), (inv[:span], lengths[:1], 0, None))
    mid2, mid3, tail2, out = together(mid2, mid3, tail2, out)
    parts = [(tails, 0, half), (mid1, 0, half)], [(tails, half, half), (mid3, 0, half)], [(tail2, 0, half), (mid2, 0, half)]
    return stage(parts, choose((1, 1), (3, 1), (2, 1)), weights, (acc, span), (inv[span:], lengths[1:], span, out))


def solution(mesh):
    fine = Mesh(mesh.devices.reshape(2, 4, 2, 4, 2), ("zh", "x", "c", "y", "zl"))
    dp, tp = ("zh", "x", "c"), ("y", "zl")
    in_specs = (P(dp, tp), P(), P(dp), P(dp, tp), P(dp, tp, None, None))
    return jax.shard_map(local, mesh=fine, in_specs=in_specs, out_specs=P(dp, tp), check_vma=False)
```

```python
import jax
import jax.numpy as jnp
from jax import lax
from jax.experimental import pallas as pl
from jax.experimental.pallas import tpu as pltpu
from jax.sharding import Mesh, PartitionSpec as P

LOG2E = 1.4426950408889634
HEAD = 128
GROUPS = 8
EPS = 1e-05


def ring(a, axis, sign=1):
    perm = []
    for c in range(2):
        for i in range(4):
            j = (i + sign) % 4 if c == 0 else (i - sign) % 4
            if axis == "y":
                perm.append((c * 4 + i, c * 4 + j))
            else:
                perm.append((i * 2 + c, j * 2 + c))
    return lax.ppermute(a, ("c", "y") if axis == "y" else ("x", "c"), perm)


def swap(a, axis):
    return lax.ppermute(a, axis, [(0, 1), (1, 0)])


def squares(a):
    wide = a.astype(jnp.float32)
    return jnp.sum(wide * wide, axis=-1)


def behind(a, *others):
    return lax.optimization_barrier((a, *others))[0]


def together(*arrays):
    return lax.optimization_barrier(arrays)


def attend_block(acc, base, inv, length, out_ref):
    span = acc.shape[0]
    half = span // 2
    factor = LOG2E * HEAD**-0.5
    at_k, at_v = GROUPS * HEAD, (GROUPS + 1) * HEAD
    k = ((acc[:, at_k : at_k + HEAD] + base[:, at_k : at_k + HEAD]) * inv).astype(jnp.bfloat16)
    v = ((acc[:, at_v : at_v + HEAD] + base[:, at_v : at_v + HEAD]) * inv).astype(jnp.bfloat16)
    v = jnp.concatenate([v, jnp.ones_like(v)], axis=1)
    for part in range(2):
        lo, hi = part * half, (part + 1) * half
        row = lax.broadcasted_iota(jnp.int32, (half, hi), 0) + lo
        col = lax.broadcasted_iota(jnp.int32, (half, hi), 1)
        bias = jnp.where((col <= row) & (col < length), 0.0, -jnp.inf)
        for g in range(GROUPS):
            at = slice(g * HEAD, (g + 1) * HEAD)
            q = ((acc[lo:hi, at] + base[lo:hi, at]) * inv[lo:hi]).astype(jnp.bfloat16)
            s = lax.dot_general(
                q, k[:hi], (((1,), (1,)), ((), ())), preferred_element_type=jnp.float32
            )
            s = s + bias
            peak = jnp.max(s, axis=-1, keepdims=True)
            e = jnp.exp2((s - peak) * factor).astype(jnp.bfloat16)
            mixed = jnp.dot(e, v[:hi], preferred_element_type=jnp.float32)
            out_ref[lo:hi, at] = (mixed[:, :HEAD] / mixed[:, HEAD:]).astype(jnp.bfloat16)


def stage(parts, sel, weights, acc_in=None, final=None):
    flat, where = [], []
    for part in parts:
        spots = []
        for array, row, count in part:
            known = [i for i, have in enumerate(flat) if have is array]
            if not known:
                flat.append(array)
            spots.append((known[0] if known else len(flat) - 1, row, count))
        where.append(spots)
    n = len(parts)
    rows = sum(count for _, _, count in where[0])
    feats = flat[0].shape[1]
    deep, width = weights[0][0].shape[0], weights[0][0].shape[1]
    stores = []
    for array, _ in weights:
        if not any(have is array for have in stores):
            stores.append(array)
    spots_w = [(next(i for i, have in enumerate(stores) if have is array), row) for array, row in weights]
    extra = [] if acc_in is None else [acc_in[0]]
    if final is not None:
        inv, length, out_row, out_old = final
        extra += [inv, length] + ([] if out_old is None else [out_old])

    def body(sel_ref, *refs):
        refs = list(refs)
        pieces = [refs.pop(0) for _ in flat]
        blocks = [refs.pop(0) for _ in stores]
        acc_ref = None if acc_in is None else refs.pop(0)
        if final is not None:
            inv_ref, length_ref = refs.pop(0), refs.pop(0)
            if out_old is not None:
                refs.pop(0)
        out_ref = refs.pop(0)
        a_buf, w_buf, acc, sem_a, sem_w, sem_c = refs[:6]

        def fetch(k, slot):
            for j, spots in enumerate(where):
                @pl.when(k == j)
                def _(spots=spots):
                    to = 0
                    for i, row, count in spots:
                        pltpu.make_async_copy(
                            pieces[i].at[pl.ds(row, count)], a_buf.at[slot, pl.ds(to, count)], sem_a.at[slot]
                        ).start()
                        to += count
            for side in range(2):
                for j, (i, row) in enumerate(spots_w):
                    @pl.when(sel_ref[2 * k + side] == j)
                    def _(i=i, row=row, side=side):
                        pltpu.make_async_copy(
                            blocks[i].at[pl.ds(row, deep)], w_buf.at[slot, pl.ds(side * deep, deep)], sem_w.at[slot]
                        ).start()

        fetch(0, 0)
        if acc_ref is not None:
            load = pltpu.make_async_copy(acc_ref.at[pl.ds(acc_in[1], rows)], refs[-1], sem_c)
            load.start()
        acc[...] = jnp.zeros_like(acc)

        def step(k, carry):
            slot = lax.rem(k, 2)

            @pl.when(k + 1 < n)
            def _():
                fetch(k + 1, 1 - slot)

            pltpu.make_async_copy(a_buf.at[slot], a_buf.at[slot], sem_a.at[slot]).wait()
            pltpu.make_async_copy(w_buf.at[slot], w_buf.at[slot], sem_w.at[slot]).wait()
            for tile in range(0, width, 256):
                at = slice(tile, tile + 256)
                acc[:, at] += jnp.dot(a_buf[slot], w_buf[slot, :, at], preferred_element_type=jnp.float32)
            return carry

        lax.fori_loop(0, n, step, 0)
        if final is None:
            save = pltpu.make_async_copy(acc, out_ref, sem_c)
        else:
            done = refs[6]
            load.wait()
            columns = []
            for i in range(out_row // HEAD, (out_row + rows) // HEAD):
                row = lax.rsqrt(inv_ref[i : i + 1, :] / (GROUPS * feats) + EPS)
                columns.append(jnp.transpose(jnp.broadcast_to(row, (HEAD, HEAD)))[:, :1])
            attend_block(acc, refs[-1], jnp.concatenate(columns, axis=0), length_ref[0], done)
            save = pltpu.make_async_copy(done, out_ref.at[pl.ds(out_row, rows)], sem_c)
        save.start()
        save.wait()

    anywhere, main = pl.BlockSpec(memory_space=pl.ANY), pl.BlockSpec(memory_space=pl.ANY)
    smem = pl.BlockSpec(memory_space=pltpu.SMEM)
    specs = [smem] + [anywhere] * (len(flat) + len(stores)) + [main] * (acc_in is not None)
    scratch = [
        pltpu.VMEM((2, rows, feats), jnp.bfloat16),
        pltpu.VMEM((2, 2 * deep, width), jnp.bfloat16),
        pltpu.VMEM((rows, width), jnp.float32),
        pltpu.SemaphoreType.DMA((2,)),
        pltpu.SemaphoreType.DMA((2,)),
        pltpu.SemaphoreType.DMA,
    ]
    aliases = {}
    flops = 2 * n * rows * feats * width
    if final is None:
        out = jax.ShapeDtypeStruct((rows, width), jnp.float32)
    else:
        specs += [pl.BlockSpec(memory_space=pltpu.VMEM), smem]
        out = jax.ShapeDtypeStruct((2 * rows, GROUPS * HEAD), jnp.bfloat16)
        scratch += [pltpu.VMEM((rows, GROUPS * HEAD), jnp.bfloat16), pltpu.VMEM((rows, width), jnp.float32)]
        flops += 6 * 10**9
        if out_old is not None:
            aliases[len(specs)] = 0
            specs.append(main)
    return pl.pallas_call(
        body,
        in_specs=specs,
        out_specs=main,
        out_shape=out,
        scratch_shapes=scratch,
        input_output_aliases=aliases,
        compiler_params=pltpu.CompilerParams(vmem_limit_bytes=56 << 20),
        cost_estimate=pl.CostEstimate(flops=flops, bytes_accessed=n * 4 * 10**6, transcendentals=0),
    )(sel, *flat, *stores, *extra)


def local(hidden, norm_gain, lengths, query_weight, keyval_weight):
    zh, x, c = lax.axis_index("zh"), lax.axis_index("x"), lax.axis_index("c")
    y, zl = lax.axis_index("y"), lax.axis_index("zl")
    rows, feats = query_weight.shape[0], hidden.shape[1]
    span = hidden.shape[0] // 2
    cut = span + span // 2

    gain = lax.dynamic_slice(norm_gain, ((zh * 8 + x * 2 + c) * rows,), (rows,))
    own = jnp.concatenate([query_weight, keyval_weight.reshape(rows, -1)], axis=1)
    own = (own.astype(jnp.float32) * gain[:, None]).astype(jnp.bfloat16)
    width = own.shape[1]

    half = span // 2
    h0, w0 = hidden, own
    def choose(side, *ones):
        step = jnp.array([k for k, _ in ones], jnp.int32)
        other = jnp.array([z for _, z in ones], jnp.int32)
        b = 2 * (jnp.where(c == 0, y - step, y + step) & 3) + (side ^ other)
        z_at, x_at = b >> 2, b & 3
        core = jnp.array([0, 1], jnp.int32)[None, :]
        k = jnp.where(core == 0, x - x_at[:, None], x_at[:, None] - x) & 3
        return (((z_at ^ zh)[:, None]) * 8 + (core ^ c) * 4 + k).reshape(-1)

    f0 = swap(w0, "zh")
    w1, w3 = ring(w0, "x"), ring(w0, "x", -1)
    h1 = ring(h0, "y")
    h_lo, h_hi = h0[:span], h0[span:]
    h3_lo = ring(h_lo, "y", -1)
    square = squares(h0)
    f0, w0, w1, w3, h0, h1, h3_lo, h_lo, h_hi, square = together(f0, w0, w1, w3, h0, h1, h3_lo, h_lo, h_hi, square)
    w2, f1 = ring(w1, "x"), ring(f0, "x")
    h3_hi = ring(h_hi, "y", -1)
    h2_lo = ring(h1[:span], "y")
    lo0 = swap(h_lo, "zl")
    others = jnp.concatenate([w0, w1, w3, f0], axis=0)
    square += squares(h1)
    h1_hi = h1[span:]
    w2, f0, f1, h0, h1, h1_hi, h2_lo, h3_hi, lo0, h_hi, square, others = together(
        w2, f0, f1, h0, h1, h1_hi, h2_lo, h3_hi, lo0, h_hi, square, others
    )
    others = swap(others, "c")
    f3, f2 = ring(f0, "x", -1), ring(f1, "x")
    h2_hi = ring(h1_hi, "y")
    hi0 = swap(h_hi, "zl")
    lo1 = ring(lo0, "y")
    more = jnp.concatenate([w2, f1], axis=0)
    side = behind(zl, h2_hi)
    picks = [
        choose(side, (0, 0), (1, 0), (2, 0), (3, 0), (0, 1)),
        choose(side, (1, 1), (2, 1), (3, 1)),
        choose(side, (1, 1), (3, 1), (2, 1)),
    ]
    square += jnp.concatenate([squares(h2_lo) + squares(h3_lo), squares(h3_hi)], axis=0)
    tail = jnp.concatenate([h1_hi[:half], h3_hi[:half]], axis=0)
    f3, f2, h2_lo, h2_hi, h3_hi, hi0, lo0, lo1, tail, square, others, more, *picks = together(
        f3, f2, h2_lo, h2_hi, h3_hi, hi0, lo0, lo1, tail, square, others, more, *picks
    )
    g2, g3, more = swap(f2, "c"), swap(f3, "c"), swap(more, "c")
    lo2, lo3 = ring(lo1, "y"), ring(lo0, "y", -1)
    mid0 = hi0[half:]
    mid1 = ring(mid0, "y")
    tails = swap(tail, "zl")
    square += jnp.concatenate([jnp.zeros_like(square[:span]), squares(h2_hi)], axis=0)
    square = square.reshape(8, -1)
    weights = [(w0, 0), (w1, 0), (w2, 0), (w3, 0), (others, 0), (others, rows), (more, 0), (others, 2 * rows)]
    weights += [(f0, 0), (f1, 0), (f2, 0), (f3, 0), (others, 3 * rows), (more, rows), (g2, 0), (g3, 0)]

    parts = [(h0, 0, 2 * span)], [(h1, 0, 2 * span)], [(h2_lo, 0, span), (h2_hi, 0, span)], [(h3_lo, 0, span), (h3_hi, 0, span)]
    parts += ([(lo0, 0, span), (hi0, 0, span)],)
    acc = stage(parts, picks[0], weights)
    tail = h2_hi[:half]
    lo2, lo3, mid0, mid1, tails, tail, acc, square = together(lo2, lo3, mid0, mid1, tails, tail, acc, square)
    square += swap(square, "zl")
    mid2, mid3 = ring(mid1, "y"), ring(mid0, "y", -1)
    tail2 = swap(tail, "zl")
    parts = [(lo1, 0, span)], [(lo2, 0, span)], [(lo3, 0, span)]
    out = stage(parts, picks[1], weights, (acc, 0), (square, lengths[:1], 0, None))
    mid2, mid3, tail2, out = together(mid2, mid3, tail2, out)
    parts = [(tails, 0, half), (mid1, 0, half)], [(tails, half, half), (mid3, 0, half)], [(tail2, 0, half), (mid2, 0, half)]
    return stage(parts, picks[2], weights, (acc, span), (square, lengths[1:], span, out))


def solution(mesh):
    fine = Mesh(mesh.devices.reshape(2, 4, 2, 4, 2), ("zh", "x", "c", "y", "zl"))
    dp, tp = ("zh", "x", "c"), ("y", "zl")
    in_specs = (P(dp, tp), P(), P(dp), P(dp, tp), P(dp, tp, None, None))
    return jax.shard_map(local, mesh=fine, in_specs=in_specs, out_specs=P(dp, tp), check_vma=False)
```

```python
import jax
import jax.numpy as jnp
from jax import lax
from jax.experimental import pallas as pl
from jax.experimental.pallas import tpu as pltpu
from jax.sharding import Mesh, PartitionSpec as P

LOG2E = 1.4426950408889634
HEAD = 128
GROUPS = 8
EPS = 1e-05


def ring(a, axis, sign=1):
    perm = []
    for c in range(2):
        for i in range(4):
            j = (i + sign) % 4 if c == 0 else (i - sign) % 4
            if axis == "y":
                perm.append((c * 4 + i, c * 4 + j))
            else:
                perm.append((i * 2 + c, j * 2 + c))
    return lax.ppermute(a, ("c", "y") if axis == "y" else ("x", "c"), perm)


def swap(a, axis):
    return lax.ppermute(a, axis, [(0, 1), (1, 0)])


def squares(a):
    wide = a.astype(jnp.float32)
    return jnp.sum(wide * wide, axis=-1)


def behind(a, *others):
    return lax.optimization_barrier((a, *others))[0]


def together(*arrays):
    return lax.optimization_barrier(arrays)


def attend_block(acc, base, inv, length, out_ref):
    span = acc.shape[0]
    half = span // 2
    factor = LOG2E * HEAD**-0.5
    at_k, at_v = GROUPS * HEAD, (GROUPS + 1) * HEAD
    k = ((acc[:, at_k : at_k + HEAD] + base[:, at_k : at_k + HEAD]) * inv).astype(jnp.bfloat16)
    v = ((acc[:, at_v : at_v + HEAD] + base[:, at_v : at_v + HEAD]) * inv).astype(jnp.bfloat16)
    v = jnp.concatenate([v, jnp.ones_like(v)], axis=1)
    for part in range(2):
        lo, hi = part * half, (part + 1) * half
        row = lax.broadcasted_iota(jnp.int32, (half, hi), 0) + lo
        col = lax.broadcasted_iota(jnp.int32, (half, hi), 1)
        bias = jnp.where((col <= row) & (col < length), 0.0, -jnp.inf)
        for g in range(GROUPS):
            at = slice(g * HEAD, (g + 1) * HEAD)
            q = ((acc[lo:hi, at] + base[lo:hi, at]) * inv[lo:hi]).astype(jnp.bfloat16)
            s = lax.dot_general(
                q, k[:hi], (((1,), (1,)), ((), ())), preferred_element_type=jnp.float32
            )
            s = s + bias
            peak = jnp.max(s, axis=-1, keepdims=True)
            e = jnp.exp2((s - peak) * factor).astype(jnp.bfloat16)
            mixed = jnp.dot(e, v[:hi], preferred_element_type=jnp.float32)
            out_ref[lo:hi, at] = (mixed[:, :HEAD] / mixed[:, HEAD:]).astype(jnp.bfloat16)


def stage(parts, sel, weights, acc_in=None, final=None):
    flat, where = [], []
    for part in parts:
        spots = []
        for array, row, count in part:
            known = [i for i, have in enumerate(flat) if have is array]
            if not known:
                flat.append(array)
            spots.append((known[0] if known else len(flat) - 1, row, count))
        where.append(spots)
    n = len(parts)
    rows = sum(count for _, _, count in where[0])
    feats = flat[0].shape[1]
    deep, width = weights[0][0].shape[0], weights[0][0].shape[1]
    stores = []
    for array, _ in weights:
        if not any(have is array for have in stores):
            stores.append(array)
    spots_w = [(next(i for i, have in enumerate(stores) if have is array), row) for array, row in weights]
    extra = [] if acc_in is None else [acc_in[0]]
    if final is not None:
        inv, length, out_row, out_old = final
        extra += [inv, length] + ([] if out_old is None else [out_old])

    def body(sel_ref, *refs):
        refs = list(refs)
        pieces = [refs.pop(0) for _ in flat]
        blocks = [refs.pop(0) for _ in stores]
        acc_ref = None if acc_in is None else refs.pop(0)
        if final is not None:
            inv_ref, length_ref = refs.pop(0), refs.pop(0)
            if out_old is not None:
                refs.pop(0)
        out_ref = refs.pop(0)
        a_buf, w_buf, acc, sem_a, sem_w, sem_c = refs[:6]

        def fetch(k, slot):
            for j, spots in enumerate(where):
                @pl.when(k == j)
                def _(spots=spots):
                    to = 0
                    for i, row, count in spots:
                        pltpu.make_async_copy(
                            pieces[i].at[pl.ds(row, count)], a_buf.at[slot, pl.ds(to, count)], sem_a.at[slot]
                        ).start()
                        to += count
            for side in range(2):
                for j, (i, row) in enumerate(spots_w):
                    @pl.when(sel_ref[2 * k + side] == j)
                    def _(i=i, row=row, side=side):
                        pltpu.make_async_copy(
                            blocks[i].at[pl.ds(row, deep)], w_buf.at[slot, pl.ds(side * deep, deep)], sem_w.at[slot]
                        ).start()

        fetch(0, 0)
        if acc_ref is not None:
            load = pltpu.make_async_copy(acc_ref.at[pl.ds(acc_in[1], rows)], refs[-1], sem_c)
            load.start()
        acc[...] = jnp.zeros_like(acc)

        def step(k, carry):
            slot = lax.rem(k, 2)

            @pl.when(k + 1 < n)
            def _():
                fetch(k + 1, 1 - slot)

            pltpu.make_async_copy(a_buf.at[slot], a_buf.at[slot], sem_a.at[slot]).wait()
            pltpu.make_async_copy(w_buf.at[slot], w_buf.at[slot], sem_w.at[slot]).wait()
            for tile in range(0, width, 256):
                at = slice(tile, tile + 256)
                acc[:, at] += jnp.dot(a_buf[slot], w_buf[slot, :, at], preferred_element_type=jnp.float32)
            return carry

        lax.fori_loop(0, n, step, 0)
        if final is None:
            save = pltpu.make_async_copy(acc, out_ref, sem_c)
        else:
            done = refs[6]
            load.wait()
            columns = []
            for i in range(out_row // HEAD, (out_row + rows) // HEAD):
                row = lax.rsqrt(inv_ref[i : i + 1, :] / (GROUPS * feats) + EPS)
                columns.append(jnp.transpose(jnp.broadcast_to(row, (HEAD, HEAD)))[:, :1])
            attend_block(acc, refs[-1], jnp.concatenate(columns, axis=0), length_ref[0], done)
            save = pltpu.make_async_copy(done, out_ref.at[pl.ds(out_row, rows)], sem_c)
        save.start()
        save.wait()

    anywhere, main = pl.BlockSpec(memory_space=pl.ANY), pl.BlockSpec(memory_space=pl.ANY)
    smem = pl.BlockSpec(memory_space=pltpu.SMEM)
    specs = [smem] + [anywhere] * (len(flat) + len(stores)) + [main] * (acc_in is not None)
    scratch = [
        pltpu.VMEM((2, rows, feats), jnp.bfloat16),
        pltpu.VMEM((2, 2 * deep, width), jnp.bfloat16),
        pltpu.VMEM((rows, width), jnp.float32),
        pltpu.SemaphoreType.DMA((2,)),
        pltpu.SemaphoreType.DMA((2,)),
        pltpu.SemaphoreType.DMA,
    ]
    aliases = {}
    flops = 2 * n * rows * feats * width
    if final is None:
        out = jax.ShapeDtypeStruct((rows, width), jnp.float32)
    else:
        specs += [pl.BlockSpec(memory_space=pltpu.VMEM), smem]
        out = jax.ShapeDtypeStruct((2 * rows, GROUPS * HEAD), jnp.bfloat16)
        scratch += [pltpu.VMEM((rows, GROUPS * HEAD), jnp.bfloat16), pltpu.VMEM((rows, width), jnp.float32)]
        flops += 6 * 10**9
        if out_old is not None:
            aliases[len(specs)] = 0
            specs.append(main)
    return pl.pallas_call(
        body,
        in_specs=specs,
        out_specs=main,
        out_shape=out,
        scratch_shapes=scratch,
        input_output_aliases=aliases,
        compiler_params=pltpu.CompilerParams(vmem_limit_bytes=56 << 20),
        cost_estimate=pl.CostEstimate(flops=flops, bytes_accessed=n * 4 * 10**6, transcendentals=0),
    )(sel, *flat, *stores, *extra)


def local(hidden, norm_gain, lengths, query_weight, keyval_weight):
    zh, x, c = lax.axis_index("zh"), lax.axis_index("x"), lax.axis_index("c")
    y, zl = lax.axis_index("y"), lax.axis_index("zl")
    rows, feats = query_weight.shape[0], hidden.shape[1]
    span = hidden.shape[0] // 2
    cut = span + span // 2

    gain = lax.dynamic_slice(norm_gain, ((zh * 8 + x * 2 + c) * rows,), (rows,))
    own = jnp.concatenate([query_weight, keyval_weight.reshape(rows, -1)], axis=1)
    own = (own.astype(jnp.float32) * gain[:, None]).astype(jnp.bfloat16)
    width = own.shape[1]

    half = span // 2
    h0, w0 = hidden, own
    def choose(side, *ones):
        step = jnp.array([k for k, _ in ones], jnp.int32)
        other = jnp.array([z for _, z in ones], jnp.int32)
        b = 2 * (jnp.where(c == 0, y - step, y + step) & 3) + (side ^ other)
        z_at, x_at = b >> 2, b & 3
        core = jnp.array([0, 1], jnp.int32)[None, :]
        k = jnp.where(core == 0, x - x_at[:, None], x_at[:, None] - x) & 3
        return (((z_at ^ zh)[:, None]) * 8 + (core ^ c) * 4 + k).reshape(-1)

    w1, w3 = ring(w0, "x"), ring(w0, "x", -1)
    f0 = swap(w0, "zh")
    h1 = ring(h0, "y")
    h_lo, h_hi = h0[:span], h0[span:]
    h3_lo = ring(h_lo, "y", -1)
    square = squares(h0)
    f0, w0, w1, w3, h0, h1, h3_lo, h_lo, h_hi, square = together(f0, w0, w1, w3, h0, h1, h3_lo, h_lo, h_hi, square)
    w2, f1 = ring(w1, "x"), ring(f0, "x")
    h3_hi = ring(h_hi, "y", -1)
    h2_lo = ring(h1[:span], "y")
    lo0 = swap(h_lo, "zl")
    others = jnp.concatenate([w0, w1, w3, f0], axis=0)
    square += squares(h1)
    h1_hi = h1[span:]
    w2, f0, f1, h0, h1, h1_hi, h2_lo, h3_hi, lo0, h_hi, square, others = together(
        w2, f0, f1, h0, h1, h1_hi, h2_lo, h3_hi, lo0, h_hi, square, others
    )
    others = swap(others, "c")
    f3, f2 = ring(f0, "x", -1), ring(f1, "x")
    h2_hi = ring(h1_hi, "y")
    hi0 = swap(h_hi, "zl")
    lo1 = ring(lo0, "y")
    more = jnp.concatenate([w2, f1], axis=0)
    side = behind(zl, h2_hi)
    picks = [
        choose(side, (0, 0), (1, 0), (2, 0), (3, 0), (0, 1)),
        choose(side, (1, 1), (2, 1), (3, 1)),
        choose(side, (1, 1), (3, 1), (2, 1)),
    ]
    square += jnp.concatenate([squares(h2_lo) + squares(h3_lo), squares(h3_hi)], axis=0)
    tail = jnp.concatenate([h1_hi[:half], h3_hi[:half]], axis=0)
    f3, f2, h2_lo, h2_hi, h3_hi, hi0, lo0, lo1, tail, square, others, more, *picks = together(
        f3, f2, h2_lo, h2_hi, h3_hi, hi0, lo0, lo1, tail, square, others, more, *picks
    )
    g2, g3, more = swap(f2, "c"), swap(f3, "c"), swap(more, "c")
    lo2, lo3 = ring(lo1, "y"), ring(lo0, "y", -1)
    mid0 = hi0[half:]
    mid1 = ring(behind(mid0, g2), "y")
    tails = swap(tail, "zl")
    square += jnp.concatenate([jnp.zeros_like(square[:span]), squares(h2_hi)], axis=0)
    square = square.reshape(8, -1)
    weights = [(w0, 0), (w1, 0), (w2, 0), (w3, 0), (others, 0), (others, rows), (more, 0), (others, 2 * rows)]
    weights += [(f0, 0), (f1, 0), (f2, 0), (f3, 0), (others, 3 * rows), (more, rows), (g2, 0), (g3, 0)]

    parts = [(h0, 0, 2 * span)], [(h1, 0, 2 * span)], [(h2_lo, 0, span), (h2_hi, 0, span)], [(h3_lo, 0, span), (h3_hi, 0, span)]
    parts += ([(lo0, 0, span), (hi0, 0, span)],)
    acc = stage(parts, picks[0], weights)
    tail = h2_hi[:half]
    lo2, lo3, mid0, mid1, tails, tail, acc, square = together(lo2, lo3, mid0, mid1, tails, tail, acc, square)
    square += swap(square, "zl")
    mid2, mid3 = ring(mid1, "y"), ring(mid0, "y", -1)
    tail2 = swap(tail, "zl")
    parts = [(lo1, 0, span)], [(lo2, 0, span)], [(lo3, 0, span)]
    out = stage(parts, picks[1], weights, (acc, 0), (square, lengths[:1], 0, None))
    mid2, mid3, tail2, out = together(mid2, mid3, tail2, out)
    parts = [(tails, 0, half), (mid1, 0, half)], [(tails, half, half), (mid3, 0, half)], [(tail2, 0, half), (mid2, 0, half)]
    return stage(parts, picks[2], weights, (acc, span), (square, lengths[1:], span, out))


def solution(mesh):
    fine = Mesh(mesh.devices.reshape(2, 4, 2, 4, 2), ("zh", "x", "c", "y", "zl"))
    dp, tp = ("zh", "x", "c"), ("y", "zl")
    in_specs = (P(dp, tp), P(), P(dp), P(dp, tp), P(dp, tp, None, None))
    return jax.shard_map(local, mesh=fine, in_specs=in_specs, out_specs=P(dp, tp), check_vma=False)
```
